512 devices in a mesh: ctx: 64 (over y_lo, z, core), head: 8 (over x, y_hi).
Axes of the slice: x: 4, y: 8 (y_hi: 2, y_lo: 4; y = y_hi * 4 + y_lo), z: 8, core: 2. Of those that a mesh axis runs over, the one named last changes fastest.
Arguments:
- queries: bfloat16 [24576, 4096], P(('ctx', 'head')), may hold values from -6 to 6
- keys: bfloat16 [24576, 1024], P(('ctx', 'head')), may hold values from -6 to 6
- values: bfloat16 [24576, 1024], P(('ctx', 'head')), may hold values from -6 to 6
- output_gradient: bfloat16 [24576, 4096], P(('ctx', 'head')), may hold values from -6 to 6
- doc_lengths: int32 [64], replicated, may hold values from 1 to 1536, 24576 in all
Outputs:
- attended: bfloat16 [24576, 4096], P(('ctx', 'head'))
- query_gradient_rows: bfloat16 [24576, 4096], P(('ctx', 'head'))
- grad_keys: bfloat16 [24576, 1024], P(('ctx', 'head'))
- grad_values: bfloat16 [24576, 1024], P(('ctx', 'head'))
The draws below stay inside these ranges and needn't reach their ends.
Inputs may be any that keep to these rules, and one draw needn't show every extreme that they name: `doc_lengths`: the 64 documents are packed in order and their lengths sum to 24576; the longest is exactly 1536, so a document covers positions of at most 5 consecutive ctx indices.
All inputs are finite; a program needn't handle non-finite values.
Results may differ from the reference program's by a relative error of at most 0.034.
Values may be sent and summed in bfloat16 or wider, within the bound.
No kernel may reach another device: no remote copies, remote signals or barrier semaphores. Data moves between devices by JAX's collectives and lax.ppermute only.
A program may use at most 128 MiB of HBM per device.

```python
import math
import jax
import jax.numpy as jnp
import numpy as np
from jax import lax

QUERY_HEAD_COUNT = 32
KEY_VALUE_HEADS = 8
HEAD_SIZE = 128
CONTEXT_TOKENS = 384
REACH = 4
SEQUENCE_TOKENS = 24576
MAXDOC = 1536
NDOCS = 64


def draw_queries(key, part):
    key = jax.random.fold_in(key, 5)
    base_offset = jax.random.normal(key, (SEQUENCE_TOKENS, QUERY_HEAD_COUNT, HEAD_SIZE), jnp.float32)
    return jnp.clip(base_offset, -6.0, 6.0).reshape(SEQUENCE_TOKENS, QUERY_HEAD_COUNT * HEAD_SIZE).astype(jnp.bfloat16)


def draw_keys(key, part):
    key = jax.random.fold_in(key, 7)
    base_offset = jax.random.normal(key, (SEQUENCE_TOKENS, KEY_VALUE_HEADS, HEAD_SIZE), jnp.float32)
    return jnp.clip(base_offset, -6.0, 6.0).reshape(SEQUENCE_TOKENS, KEY_VALUE_HEADS * HEAD_SIZE).astype(jnp.bfloat16)


def steps_of(rng, dims, split, smallest, largest):
    def one(position, blocks):
        heights = jax.random.uniform(jax.random.fold_in(jax.random.fold_in(rng, 6), position), (blocks,), jnp.float32, smallest / len(split), largest / len(split))
        return jnp.repeat(jnp.exp(heights), dims[position] // blocks).reshape((-1,) + (1,) * (len(dims) - position - 1))

    gain = one(*split[0])
    for cut in split[1:]:
        gain = gain * one(*cut)
    return gain


def length_profile(count, total, limit, skew):
    loads = [(1 << 20) // math.isqrt(standing ** skew) + 1 for standing in range(2, count + 1)]
    surplus, holding = total - limit - (count - 1), [1] * (count - 1)
    while surplus > 0:
        free = [i for i in range(count - 1) if holding[i] < limit]
        whole, remaining = sum([loads[i] for i in free]), surplus
        for i in free:
            addition = min(limit - holding[i], max(1, remaining * loads[i] // whole), surplus)
            holding[i] = holding[i] + addition
            surplus = surplus - addition
    return np.array([limit] + holding)


def uneven_parts(rng, amount, total, bound, skew):
    if amount == 2:
        one = jax.random.randint(rng, (), max(1, total - bound), min(bound, total - 1) + 1)
        return jnp.stack([one, total - one])
    sizes = jnp.asarray(length_profile(amount, total, bound, skew), jnp.int32)
    couples = (amount - 1) // 2
    giver, taker = sizes[1:1 + 2 * couples:2], sizes[2:2 + 2 * couples:2]
    margin = jnp.minimum(giver - 1, bound - taker)
    moved = jax.random.randint(jax.random.fold_in(rng, 1), (couples,), 0, 1 << 20) % (margin + 1)
    sizes = sizes.at[1:1 + 2 * couples:2].set(giver - moved).at[2:2 + 2 * couples:2].set(taker + moved)
    return sizes[jax.random.permutation(jax.random.fold_in(rng, 2), amount)]


def normal_values(key, shape, deviation, reach, pieces=(), kind=jnp.bfloat16):
    values = deviation * jax.random.normal(key, shape, jnp.float32)
    if pieces:
        values = values * steps_of(key, shape, pieces, -0.22, 0.18)
    return jnp.clip(values, -reach, reach).astype(kind)


def setup_inputs(seed: int = 0) -> dict:
    splits = jax.random.split(jax.random.key(seed), 6)
    queries = draw_queries(jax.random.fold_in(splits[5], 71), 0)
    keys = draw_keys(jax.random.fold_in(splits[5], 71), 0)
    values = normal_values(splits[2], (SEQUENCE_TOKENS, KEY_VALUE_HEADS * HEAD_SIZE), 1.0, 6.0, ((0, 512),))
    output_gradient = normal_values(splits[3], (SEQUENCE_TOKENS, QUERY_HEAD_COUNT * HEAD_SIZE), 1.0, 6.0, ((0, 512),))
    doc_lengths = uneven_parts(splits[4], NDOCS, SEQUENCE_TOKENS, MAXDOC, 2).astype(jnp.int32)
    return dict(queries=queries, keys=keys, values=values, output_gradient=output_gradient, doc_lengths=doc_lengths)


def document_ids(doc_lengths, positions):
    ends = jnp.cumsum(doc_lengths)
    return lax.optimization_barrier(jnp.sum((ends[None, :] <= positions[:, None]).astype(jnp.int32), axis=1))

def allowed(query_pos, key_pos, doc_lengths):
    same = document_ids(doc_lengths, query_pos)[:, None] == document_ids(doc_lengths, key_pos)[None, :]
    return same & (key_pos[None, :] <= query_pos[:, None]) & (key_pos[None, :] >= 0)

def rounded(array):
    return lax.optimization_barrier(array.astype(jnp.bfloat16)).astype(jnp.float32)

def reference(queries, keys, values, output_gradient, doc_lengths):
    head_group = QUERY_HEAD_COUNT // KEY_VALUE_HEADS
    scale = 1.0 / math.sqrt(HEAD_SIZE)
    token_span = REACH * CONTEXT_TOKENS
    window = token_span + CONTEXT_TOKENS
    block_list = SEQUENCE_TOKENS // CONTEXT_TOKENS
    query_block_list = queries.reshape(block_list, CONTEXT_TOKENS, KEY_VALUE_HEADS, head_group, HEAD_SIZE)
    gradient_block_list = output_gradient.reshape(block_list, CONTEXT_TOKENS, KEY_VALUE_HEADS, head_group, HEAD_SIZE)
    padding_rows = jnp.zeros((token_span, KEY_VALUE_HEADS * HEAD_SIZE), keys.dtype)
    gathered_keys = jnp.concatenate([padding_rows, keys], 0).reshape(SEQUENCE_TOKENS + token_span, KEY_VALUE_HEADS, HEAD_SIZE)
    gathered_values = jnp.concatenate([padding_rows, values], 0).reshape(SEQUENCE_TOKENS + token_span, KEY_VALUE_HEADS, HEAD_SIZE)
    starts = jnp.arange(block_list, dtype=jnp.int32) * CONTEXT_TOKENS

    def one_block(carry, inputs):
        key_gradient, value_gradient = carry
        start, query_block, grad_block = inputs
        key_win = lax.dynamic_slice_in_dim(gathered_keys, start, window, 0).astype(jnp.float32)
        value_win = lax.dynamic_slice_in_dim(gathered_values, start, window, 0).astype(jnp.float32)
        query_f = query_block.astype(jnp.float32)
        grad_f = grad_block.astype(jnp.float32)
        query_pos = start + jnp.arange(CONTEXT_TOKENS, dtype=jnp.int32)
        key_pos = start - token_span + jnp.arange(window, dtype=jnp.int32)
        mask = allowed(query_pos, key_pos, doc_lengths)
        scores = jnp.einsum('qgjd,kgd->gjqk', query_f, key_win) * scale
        top = lax.optimization_barrier(jnp.max(jnp.where(mask, scores, -jnp.inf), axis=-1, keepdims=True))
        weights = jnp.where(mask, jnp.exp(scores - top), 0.0)
        total = lax.optimization_barrier(jnp.sum(weights, axis=-1, keepdims=True))
        summed = jnp.einsum('gjqk,kgd->qgjd', rounded(weights), value_win)
        attended = (summed / jnp.transpose(total, (2, 0, 1, 3))).astype(jnp.bfloat16)
        log_total = top + jnp.log(total)
        delta = jnp.transpose(lax.optimization_barrier(jnp.sum(grad_f * attended.astype(jnp.float32), axis=-1)), (1, 2, 0))[..., None]
        probs = jnp.where(mask, jnp.exp(scores - log_total), 0.0)
        dprobs = jnp.einsum('qgjd,kgd->gjqk', grad_f, value_win)
        dscores = rounded(probs * (dprobs - delta))
        probs_b = rounded(probs)
        grad_query = jnp.einsum('gjqk,kgd->qgjd', dscores, key_win) * scale
        key_part = jnp.einsum('gjqk,qgjd->kgd', dscores, query_f) * scale
        value_part = jnp.einsum('gjqk,qgjd->kgd', probs_b, grad_f)
        key_gradient = lax.dynamic_update_slice_in_dim(key_gradient, lax.dynamic_slice_in_dim(key_gradient, start, window, 0) + key_part, start, 0)
        value_gradient = lax.dynamic_update_slice_in_dim(value_gradient, lax.dynamic_slice_in_dim(value_gradient, start, window, 0) + value_part, start, 0)
        return ((key_gradient, value_gradient), (attended, grad_query.astype(jnp.bfloat16)))
    zero_filled = jnp.zeros((SEQUENCE_TOKENS + token_span, KEY_VALUE_HEADS, HEAD_SIZE), jnp.float32)
    (key_gradient, value_gradient), (attended, query_gradient_rows) = lax.scan(one_block, (zero_filled, zero_filled), (starts, query_block_list, gradient_block_list))
    return (attended.reshape(SEQUENCE_TOKENS, QUERY_HEAD_COUNT * HEAD_SIZE), query_gradient_rows.reshape(SEQUENCE_TOKENS, QUERY_HEAD_COUNT * HEAD_SIZE), key_gradient[token_span:].reshape(SEQUENCE_TOKENS, KEY_VALUE_HEADS * HEAD_SIZE).astype(jnp.bfloat16), value_gradient[token_span:].reshape(SEQUENCE_TOKENS, KEY_VALUE_HEADS * HEAD_SIZE).astype(jnp.bfloat16))
```

```python
import math

import jax
import jax.numpy as jnp
from jax import lax
from jax.experimental import pallas as pl
from jax.experimental.pallas import tpu as pltpu
from jax.sharding import PartitionSpec as P

HEADS = 8
GROUP = 4
D = 128
ROWS = 384
SUB = 48
XS = 4
CHIP = 2 * ROWS
BACK = 2
OWN = BACK * CHIP
TK = 256
WINDOW = OWN + CHIP + TK
TQ = 128
QTILES = ROWS // TQ
LANES = TQ * GROUP
QDO = 2 * GROUP * D
SCALE = 1.0 / math.sqrt(D)
LOG2E = 1.4426950408889634
MASKED = -1e30

NT = (((1,), (1,)), ((), ()))
TN = (((0,), (0,)), ((), ()))

SMEM = pl.BlockSpec(memory_space=pltpu.SMEM)
VMEM = pl.BlockSpec(memory_space=pltpu.VMEM)


def dot(a, b):
    return jnp.dot(a, b, preferred_element_type=jnp.float32)


def dot_nt(a, b):
    return lax.dot_general(a, b, NT, preferred_element_type=jnp.float32)


def dot_tn(a, b):
    return lax.dot_general(a, b, TN, preferred_element_type=jnp.float32)


def pack_kernel(a_ref, b_ref, out_ref):
    width = a_ref.shape[1] // HEADS
    for head in range(HEADS):
        out_ref[head, :, :width] = a_ref[:, head * width : (head + 1) * width]
        out_ref[head, :, width:] = b_ref[:, head * width : (head + 1) * width]


def pack(a, b):
    width = a.shape[1] // HEADS
    return pl.pallas_call(
        pack_kernel,
        out_shape=jax.ShapeDtypeStruct((HEADS, SUB, 2 * width), jnp.bfloat16),
        in_specs=[VMEM] * 2,
        out_specs=VMEM,
        cost_estimate=pl.CostEstimate(
            flops=0, bytes_accessed=8 * HEADS * SUB * width, transcendentals=0
        ),
        name="pack",
    )(a, b)


def unpack_kernel(got_ref, a_ref, b_ref):
    width = a_ref.shape[1] // HEADS
    for head in range(HEADS):
        a_ref[:, head * width : (head + 1) * width] = got_ref[head, :, :width]
        b_ref[:, head * width : (head + 1) * width] = got_ref[head, :, width:]


def unpack(got):
    width = got.shape[2] // 2
    part = jax.ShapeDtypeStruct((SUB, HEADS * width), jnp.bfloat16)
    return pl.pallas_call(
        unpack_kernel,
        out_shape=(part, part),
        in_specs=[VMEM],
        out_specs=(VMEM, VMEM),
        cost_estimate=pl.CostEstimate(
            flops=0, bytes_accessed=8 * HEADS * SUB * width, transcendentals=0
        ),
        name="unpack",
    )(got)


def attention_kernel(half, span, start_ref, own_ref, qdo, *refs):
    kv_refs, odq, g_refs = refs[:6], refs[6], refs[7:13]
    kv, weights, weights_b, dprobs, dkv, acc_t = refs[13:]

    def stripes(j):
        return [
            (
                slice((i * XS + x) * SUB, (i * XS + x + 1) * SUB),
                pl.multiple_of(i * ROWS + (2 * x + (half[0] ^ j)) * SUB, SUB),
            )
            for i in range(2)
            for x in range(XS)
        ]

    kv[OWN + CHIP :, :] = jnp.zeros((TK, 2 * D), kv.dtype)
    for j in range(2):
        for held, place in stripes(j):
            for chip in range(BACK + 1):
                kv[pl.ds(place + OWN - chip * CHIP, SUB), :] = kv_refs[2 * chip + j][held, :]
    dkv[...] = jnp.zeros_like(dkv)
    key_iota = lax.broadcasted_iota(jnp.int32, (TK, LANES), 0)

    def query_tile(qi, _):
        rows = pl.ds(pl.multiple_of(qi * TQ, TQ), TQ)
        q = jnp.concatenate([qdo[rows, j * D : (j + 1) * D] for j in range(GROUP)], axis=0)
        do = jnp.concatenate(
            [qdo[rows, (GROUP + j) * D : (GROUP + j + 1) * D] for j in range(GROUP)], axis=0
        )
        start = start_ref[qi]
        own = own_ref[qi]
        low = span[qi] // TK
        high = span[QTILES + qi] // TK + 1
        steps = (high - low + 1) // 2

        def tiles(step):
            first = low + 2 * step
            return [pl.multiple_of((first + t) * TK, TK) for t in range(2)]

        def score(step, top):
            for base in tiles(step):
                keys = pl.ds(base, TK)
                s = dot_nt(kv[keys, :D], q)
                s = jnp.where((key_iota >= start - base) & (key_iota <= own - base), s, MASKED)
                weights[keys, :] = s
                top = jnp.maximum(top, jnp.max(s.reshape(TK // 8, 8, LANES), axis=0))
            return top

        top = lax.fori_loop(0, steps, score, jnp.full((8, LANES), MASKED, jnp.float32))
        top = jnp.max(top, axis=0, keepdims=True) * (SCALE * LOG2E)
        acc_t[...] = jnp.zeros_like(acc_t)

        def weigh(step, total):
            summed = 0.0
            for base in tiles(step):
                keys = pl.ds(base, TK)
                dprobs[keys, :] = dot_nt(kv[keys, D:], do)
                w = jnp.exp2(weights[keys, :] * (SCALE * LOG2E) - top)
                w_b = w.astype(jnp.bfloat16)
                weights_b[keys, :] = w_b
                summed += dot_tn(kv[keys, D:], w_b)
                total = total + jnp.sum(w.reshape(TK // 8, 8, LANES), axis=0)
            acc_t[...] += summed
            return total

        total = lax.fori_loop(0, steps, weigh, jnp.zeros((8, LANES), jnp.float32))
        inverse = 1.0 / jnp.sum(total, axis=0, keepdims=True)
        attended_t = (acc_t[...] * inverse).astype(jnp.bfloat16)
        delta = jnp.sum(
            do.T.astype(jnp.float32) * attended_t.astype(jnp.float32), axis=0, keepdims=True
        )
        inverse = inverse.astype(jnp.bfloat16)
        for j in range(GROUP):
            odq[rows, j * D : (j + 1) * D] = attended_t[:, j * TQ : (j + 1) * TQ].T
        acc_t[...] = jnp.zeros_like(acc_t)

        def grads(step, carry):
            summed = 0.0
            for base in tiles(step):
                keys = pl.ds(base, TK)
                probs = weights_b[keys, :] * inverse
                dscores = probs * (dprobs[keys, :] - delta).astype(jnp.bfloat16)
                summed += dot_tn(kv[keys, :D], dscores)
                dkv[keys, :D] += dot(dscores, q)
                dkv[keys, D:] += dot(probs, do)
            acc_t[...] += summed
            return carry

        lax.fori_loop(0, steps, grads, 0)
        dq_t = (acc_t[...] * SCALE).astype(jnp.bfloat16)
        for j in range(GROUP):
            odq[rows, (GROUP + j) * D : (GROUP + j + 1) * D] = dq_t[:, j * TQ : (j + 1) * TQ].T
        return 0

    lax.fori_loop(0, QTILES, query_tile, 0)
    for j in range(2):
        for held, place in stripes(j):
            for chip in range(BACK + 1):
                part = dkv[pl.ds(place + OWN - chip * CHIP, SUB), :]
                part = jnp.concatenate([part[:, :D] * SCALE, part[:, D:]], axis=1)
                ref = g_refs[2 * chip + j]
                ref[held, :] = part.astype(ref.dtype)


def attention(half, span, start, own, qdo, blocks):
    part = jax.ShapeDtypeStruct((ROWS, 2 * D), jnp.bfloat16)
    kept = jax.ShapeDtypeStruct((ROWS, 2 * D), jnp.float32)
    return pl.pallas_call(
        attention_kernel,
        out_shape=(jax.ShapeDtypeStruct((ROWS, QDO), jnp.bfloat16), kept, kept) + (part,) * 4,
        in_specs=[SMEM, SMEM] + [VMEM] * 9,
        out_specs=(VMEM,) * 7,
        scratch_shapes=[
            pltpu.VMEM((WINDOW, 2 * D), jnp.bfloat16),
            pltpu.VMEM((WINDOW, LANES), jnp.float32),
            pltpu.VMEM((WINDOW, LANES), jnp.bfloat16),
            pltpu.VMEM((WINDOW, LANES), jnp.float32),
            pltpu.VMEM((WINDOW, 2 * D), jnp.float32),
            pltpu.VMEM((D, LANES), jnp.float32),
        ],
        compiler_params=pltpu.CompilerParams(vmem_limit_bytes=44 << 20),
        cost_estimate=pl.CostEstimate(
            flops=6 * 2 * D * ROWS * GROUP * 1200, bytes_accessed=4 << 20, transcendentals=0
        ),
        name="attention",
    )(half, span, start, own, qdo, *blocks)


def query_spans(doc_lengths, place, half):
    ends = jnp.cumsum(doc_lengths)
    row = jnp.arange(ROWS, dtype=jnp.int32)
    stripe = row // SUB
    own = OWN + (stripe // XS) * ROWS + (2 * (stripe % XS) + half) * SUB + row % SUB
    base = (place // 2) * CHIP - OWN
    pos = own + base
    start = jnp.max(jnp.where(ends[None, :] <= pos[:, None], ends[None, :], 0), axis=1) - base
    span = jnp.concatenate([start[::TQ], own[TQ - 1 :: TQ]])

    def tiled(v):
        v = jnp.broadcast_to(v.reshape(QTILES, 1, 1, TQ), (QTILES, 1, GROUP, TQ))
        return v.reshape(QTILES, 1, LANES)

    return span, tiled(start), tiled(own)


CTX = ("y_low", "z", "core")


def exchanged(pieces):
    return lax.all_to_all(pieces, ("core", "x"), split_axis=0, concat_axis=0, tiled=True)


def shifted(shard, by):
    peers = lax.axis_size(CTX)
    pairs = [(i, i + by) for i in range(peers) if 0 <= i + by < peers]
    return lax.ppermute(shard, CTX, pairs)


def half_swapped(shard):
    return lax.ppermute(shard, "y_high", [(0, 1), (1, 0)])


def local(queries, keys, values, output_gradient, doc_lengths):
    place = lax.axis_index(CTX)
    half = lax.axis_index("y_high").astype(jnp.int32)
    own = exchanged(pack(keys, values)).reshape(ROWS, 2 * D)
    theirs = half_swapped(own)
    own1, own2 = shifted(own, 2), shifted(own, 4)
    qdo = exchanged(pack(queries, output_gradient)).reshape(ROWS, QDO)
    theirs1, theirs2 = shifted(theirs, 2), shifted(theirs, 4)
    span, start, own_pos = query_spans(doc_lengths, place, half)

    blocks = (own, theirs, own1, theirs1, own2, theirs2)
    odq, g0, h0, g1, h1, g2, h2 = attention(half.reshape(1), span, start, own_pos, qdo, blocks)
    h1, h2 = shifted(h1, -2), shifted(h2, -4)
    odq_rows = exchanged(odq.reshape(HEADS, SUB, QDO))
    theirs = (h0 + h1.astype(jnp.float32) + h2.astype(jnp.float32)).astype(jnp.bfloat16)
    theirs, g1, g2 = lax.optimization_barrier((theirs, g1, g2))
    got = half_swapped(theirs).astype(jnp.float32)
    g1, g2 = shifted(g1, -2), shifted(g2, -4)
    total = g0 + g1.astype(jnp.float32) + g2.astype(jnp.float32) + got
    odq_rows, total = lax.optimization_barrier((odq_rows, total.astype(jnp.bfloat16)))
    dkv_rows = exchanged(total.reshape(HEADS, SUB, 2 * D))
    return (*unpack(odq_rows), *unpack(dkv_rows))


def solution(mesh):
    mesh = jax.sharding.Mesh(
        mesh.devices.reshape(4, 8, 2, 4, 2), ("y_low", "z", "core", "x", "y_high")
    )
    spec = P(("y_low", "z", "core", "x", "y_high"), None)
    return jax.shard_map(
        local,
        mesh=mesh,
        in_specs=(spec, spec, spec, spec, P()),
        out_specs=(spec, spec, spec, spec),
        check_vma=False,
    )
```

```python
import math

import jax
import jax.numpy as jnp
from jax import lax
from jax.experimental import pallas as pl
from jax.experimental.pallas import tpu as pltpu
from jax.sharding import PartitionSpec as P

HEADS = 8
GROUP = 4
D = 128
ROWS = 384
SUB = 48
XS = 4
CHIP = 2 * ROWS
BACK = 2
OWN = BACK * CHIP
TK = 256
STEP = 2 * TK
WINDOW = OWN + CHIP + TK
TQ = 128
QTILES = ROWS // TQ
LANES = TQ * GROUP
QDO = 2 * GROUP * D
SCALE = 1.0 / math.sqrt(D)
LOG2E = 1.4426950408889634
MASKED = -1e30

NT = (((1,), (1,)), ((), ()))
TN = (((0,), (0,)), ((), ()))

SMEM = pl.BlockSpec(memory_space=pltpu.SMEM)
VMEM = pl.BlockSpec(memory_space=pltpu.VMEM)


def dot(a, b):
    return jnp.dot(a, b, preferred_element_type=jnp.float32)


def dot_nt(a, b):
    return lax.dot_general(a, b, NT, preferred_element_type=jnp.float32)


def dot_tn(a, b):
    return lax.dot_general(a, b, TN, preferred_element_type=jnp.float32)


def pack_kernel(a_ref, b_ref, out_ref):
    width = a_ref.shape[1] // HEADS
    for head in range(HEADS):
        out_ref[head, :, :width] = a_ref[:, head * width : (head + 1) * width]
        out_ref[head, :, width:] = b_ref[:, head * width : (head + 1) * width]


def pack(a, b):
    width = a.shape[1] // HEADS
    return pl.pallas_call(
        pack_kernel,
        out_shape=jax.ShapeDtypeStruct((HEADS, SUB, 2 * width), jnp.bfloat16),
        in_specs=[VMEM] * 2,
        out_specs=VMEM,
        cost_estimate=pl.CostEstimate(
            flops=0, bytes_accessed=8 * HEADS * SUB * width, transcendentals=0
        ),
        name="pack",
    )(a, b)


def unpack_kernel(got_ref, a_ref, b_ref):
    width = a_ref.shape[1] // HEADS
    for head in range(HEADS):
        a_ref[:, head * width : (head + 1) * width] = got_ref[head, :, :width]
        b_ref[:, head * width : (head + 1) * width] = got_ref[head, :, width:]


def unpack(got):
    width = got.shape[2] // 2
    part = jax.ShapeDtypeStruct((SUB, HEADS * width), jnp.bfloat16)
    return pl.pallas_call(
        unpack_kernel,
        out_shape=(part, part),
        in_specs=[VMEM],
        out_specs=(VMEM, VMEM),
        cost_estimate=pl.CostEstimate(
            flops=0, bytes_accessed=8 * HEADS * SUB * width, transcendentals=0
        ),
        name="unpack",
    )(got)


def attention_kernel(half, span, start_ref, own_ref, qdo, *refs):
    kv_refs, odq, g_refs = refs[:6], refs[6], refs[7:13]
    kv, weights, weights_b, dprobs, dkv, acc_t = refs[13:]

    def stripes(j):
        return [
            (
                slice((i * XS + x) * SUB, (i * XS + x + 1) * SUB),
                pl.multiple_of(i * ROWS + (2 * x + (half[0] ^ j)) * SUB, SUB),
            )
            for i in range(2)
            for x in range(XS)
        ]

    kv[OWN + CHIP :, :] = jnp.zeros((TK, 2 * D), kv.dtype)
    for j in range(2):
        for held, place in stripes(j):
            for chip in range(BACK + 1):
                kv[pl.ds(place + OWN - chip * CHIP, SUB), :] = kv_refs[2 * chip + j][held, :]
    dkv[...] = jnp.zeros_like(dkv)
    key_iota = lax.broadcasted_iota(jnp.int32, (STEP, LANES), 0)

    def query_tile(qi, _):
        rows = pl.ds(pl.multiple_of(qi * TQ, TQ), TQ)
        q = jnp.concatenate([qdo[rows, j * D : (j + 1) * D] for j in range(GROUP)], axis=0)
        do = jnp.concatenate(
            [qdo[rows, (GROUP + j) * D : (GROUP + j + 1) * D] for j in range(GROUP)], axis=0
        )
        start = start_ref[qi]
        own = own_ref[qi]
        low = span[qi] // TK
        high = span[QTILES + qi] // TK + 1
        steps = (high - low + 1) // 2

        def place(step):
            return pl.multiple_of((low + 2 * step) * TK, TK)

        def score(step, top):
            base = place(step)
            keys = pl.ds(base, STEP)
            s = dot_nt(kv[keys, :D], q)
            s = jnp.where((key_iota >= start - base) & (key_iota <= own - base), s, MASKED)
            weights[keys, :] = s
            return jnp.maximum(top, jnp.max(s.reshape(STEP // 8, 8, LANES), axis=0))

        top = lax.fori_loop(0, steps, score, jnp.full((8, LANES), MASKED, jnp.float32))
        top = jnp.max(top, axis=0, keepdims=True) * (SCALE * LOG2E)
        acc_t[...] = jnp.zeros_like(acc_t)

        def weigh(step, total):
            keys = pl.ds(place(step), STEP)
            dprobs[keys, :] = dot_nt(kv[keys, D:], do)
            w = jnp.exp2(weights[keys, :] * (SCALE * LOG2E) - top)
            w_b = w.astype(jnp.bfloat16)
            weights_b[keys, :] = w_b
            acc_t[...] += dot_tn(kv[keys, D:], w_b)
            return total + jnp.sum(w.reshape(STEP // 8, 8, LANES), axis=0)

        total = lax.fori_loop(0, steps, weigh, jnp.zeros((8, LANES), jnp.float32))
        inverse = 1.0 / jnp.sum(total, axis=0, keepdims=True)
        attended_t = (acc_t[...] * inverse).astype(jnp.bfloat16)
        delta = jnp.sum(
            do.T.astype(jnp.float32) * attended_t.astype(jnp.float32), axis=0, keepdims=True
        )
        inverse = inverse.astype(jnp.bfloat16)
        for j in range(GROUP):
            odq[rows, j * D : (j + 1) * D] = attended_t[:, j * TQ : (j + 1) * TQ].T
        acc_t[...] = jnp.zeros_like(acc_t)

        def grads(step, carry):
            keys = pl.ds(place(step), STEP)
            probs = weights_b[keys, :] * inverse
            dscores = probs * (dprobs[keys, :] - delta).astype(jnp.bfloat16)
            acc_t[...] += dot_tn(kv[keys, :D], dscores)
            dkv[keys, :D] += dot(dscores, q)
            dkv[keys, D:] += dot(probs, do)
            return carry

        lax.fori_loop(0, steps, grads, 0)
        dq_t = (acc_t[...] * SCALE).astype(jnp.bfloat16)
        for j in range(GROUP):
            odq[rows, (GROUP + j) * D : (GROUP + j + 1) * D] = dq_t[:, j * TQ : (j + 1) * TQ].T
        return 0

    lax.fori_loop(0, QTILES, query_tile, 0)
    for j in range(2):
        for held, place in stripes(j):
            for chip in range(BACK + 1):
                part = dkv[pl.ds(place + OWN - chip * CHIP, SUB), :]
                part = jnp.concatenate([part[:, :D] * SCALE, part[:, D:]], axis=1)
                ref = g_refs[2 * chip + j]
                ref[held, :] = part.astype(ref.dtype)


def attention(half, span, start, own, qdo, blocks):
    part = jax.ShapeDtypeStruct((ROWS, 2 * D), jnp.bfloat16)
    kept = jax.ShapeDtypeStruct((ROWS, 2 * D), jnp.float32)
    return pl.pallas_call(
        attention_kernel,
        out_shape=(jax.ShapeDtypeStruct((ROWS, QDO), jnp.bfloat16), kept, kept) + (part,) * 4,
        in_specs=[SMEM, SMEM] + [VMEM] * 9,
        out_specs=(VMEM,) * 7,
        scratch_shapes=[
            pltpu.VMEM((WINDOW, 2 * D), jnp.bfloat16),
            pltpu.VMEM((WINDOW, LANES), jnp.float32),
            pltpu.VMEM((WINDOW, LANES), jnp.bfloat16),
            pltpu.VMEM((WINDOW, LANES), jnp.float32),
            pltpu.VMEM((WINDOW, 2 * D), jnp.float32),
            pltpu.VMEM((D, LANES), jnp.float32),
        ],
        compiler_params=pltpu.CompilerParams(vmem_limit_bytes=44 << 20),
        cost_estimate=pl.CostEstimate(
            flops=6 * 2 * D * ROWS * GROUP * 1200, bytes_accessed=4 << 20, transcendentals=0
        ),
        name="attention",
    )(half, span, start, own, qdo, *blocks)


def query_spans(doc_lengths, place, half):
    ends = jnp.cumsum(doc_lengths)
    row = jnp.arange(ROWS, dtype=jnp.int32)
    stripe = row // SUB
    own = OWN + (stripe // XS) * ROWS + (2 * (stripe % XS) + half) * SUB + row % SUB
    base = (place // 2) * CHIP - OWN
    pos = own + base
    start = jnp.max(jnp.where(ends[None, :] <= pos[:, None], ends[None, :], 0), axis=1) - base
    span = jnp.concatenate([start[::TQ], own[TQ - 1 :: TQ]])

    def tiled(v):
        v = jnp.broadcast_to(v.reshape(QTILES, 1, 1, TQ), (QTILES, 1, GROUP, TQ))
        return v.reshape(QTILES, 1, LANES)

    return span, tiled(start), tiled(own)


CTX = ("y_low", "z", "core")


def exchanged(pieces):
    return lax.all_to_all(pieces, ("core", "x"), split_axis=0, concat_axis=0, tiled=True)


def shifted(shard, by):
    peers = lax.axis_size(CTX)
    pairs = [(i, i + by) for i in range(peers) if 0 <= i + by < peers]
    return lax.ppermute(shard, CTX, pairs)


def half_swapped(shard):
    return lax.ppermute(shard, "y_high", [(0, 1), (1, 0)])


def local(queries, keys, values, output_gradient, doc_lengths):
    place = lax.axis_index(CTX)
    half = lax.axis_index("y_high").astype(jnp.int32)
    own = exchanged(pack(keys, values)).reshape(ROWS, 2 * D)
    theirs = half_swapped(own)
    own1, own2 = shifted(own, 2), shifted(own, 4)
    qdo = exchanged(pack(queries, output_gradient)).reshape(ROWS, QDO)
    theirs1, theirs2 = shifted(theirs, 2), shifted(theirs, 4)
    span, start, own_pos = query_spans(doc_lengths, place, half)

    blocks = (own, theirs, own1, theirs1, own2, theirs2)
    odq, g0, h0, g1, h1, g2, h2 = attention(half.reshape(1), span, start, own_pos, qdo, blocks)
    h1, h2 = shifted(h1, -2), shifted(h2, -4)
    odq_rows = exchanged(odq.reshape(HEADS, SUB, QDO))
    theirs = (h0 + h1.astype(jnp.float32) + h2.astype(jnp.float32)).astype(jnp.bfloat16)
    got = half_swapped(theirs).astype(jnp.float32)
    g1, g2 = shifted(g1, -2), shifted(g2, -4)
    total = g0 + g1.astype(jnp.float32) + g2.astype(jnp.float32) + got
    odq_rows, total = lax.optimization_barrier((odq_rows, total.astype(jnp.bfloat16)))
    dkv_rows = exchanged(total.reshape(HEADS, SUB, 2 * D))
    return (*unpack(odq_rows), *unpack(dkv_rows))


def solution(mesh):
    mesh = jax.sharding.Mesh(
        mesh.devices.reshape(4, 8, 2, 4, 2), ("y_low", "z", "core", "x", "y_high")
    )
    spec = P(("y_low", "z", "core", "x", "y_high"), None)
    return jax.shard_map(
        local,
        mesh=mesh,
        in_specs=(spec, spec, spec, spec, P()),
        out_specs=(spec, spec, spec, spec),
        check_vma=False,
    )
```

```python
import math

import jax
import jax.numpy as jnp
from jax import lax
from jax.experimental import pallas as pl
from jax.experimental.pallas import tpu as pltpu
from jax.sharding import PartitionSpec as P

HEADS = 8
GROUP = 4
D = 128
ROWS = 384
SUB = 48
XS = 4
CHIP = 2 * ROWS
BACK = 2
OWN = BACK * CHIP
TK = 256
STEP = 2 * TK
WINDOW = OWN + CHIP + STEP
TQ = 128
QTILES = ROWS // TQ
LANES = TQ * GROUP
QDO = 2 * GROUP * D
SCALE = 1.0 / math.sqrt(D)
LOG2E = 1.4426950408889634
MASKED = -1e30

NT = (((1,), (1,)), ((), ()))
TN = (((0,), (0,)), ((), ()))

SMEM = pl.BlockSpec(memory_space=pltpu.SMEM)
VMEM = pl.BlockSpec(memory_space=pltpu.VMEM)


def dot(a, b):
    return jnp.dot(a, b, preferred_element_type=jnp.float32)


def dot_nt(a, b):
    return lax.dot_general(a, b, NT, preferred_element_type=jnp.float32)


def dot_tn(a, b):
    return lax.dot_general(a, b, TN, preferred_element_type=jnp.float32)


def pack_kernel(a_ref, b_ref, out_ref):
    width = a_ref.shape[1] // HEADS
    for head in range(HEADS):
        out_ref[head, :, :width] = a_ref[:, head * width : (head + 1) * width]
        out_ref[head, :, width:] = b_ref[:, head * width : (head + 1) * width]


def pack(a, b):
    width = a.shape[1] // HEADS
    return pl.pallas_call(
        pack_kernel,
        out_shape=jax.ShapeDtypeStruct((HEADS, SUB, 2 * width), jnp.bfloat16),
        in_specs=[VMEM] * 2,
        out_specs=VMEM,
        cost_estimate=pl.CostEstimate(
            flops=0, bytes_accessed=8 * HEADS * SUB * width, transcendentals=0
        ),
        name="pack",
    )(a, b)


def unpack_kernel(got_ref, a_ref, b_ref):
    width = a_ref.shape[1] // HEADS
    for head in range(HEADS):
        a_ref[:, head * width : (head + 1) * width] = got_ref[head, :, :width]
        b_ref[:, head * width : (head + 1) * width] = got_ref[head, :, width:]


def unpack(got):
    width = got.shape[2] // 2
    part = jax.ShapeDtypeStruct((SUB, HEADS * width), jnp.bfloat16)
    return pl.pallas_call(
        unpack_kernel,
        out_shape=(part, part),
        in_specs=[VMEM],
        out_specs=(VMEM, VMEM),
        cost_estimate=pl.CostEstimate(
            flops=0, bytes_accessed=8 * HEADS * SUB * width, transcendentals=0
        ),
        name="unpack",
    )(got)


def attention_kernel(half, span, start_ref, own_ref, qdo, *refs):
    kv_refs, odq, g_refs = refs[:6], refs[6], refs[7:13]
    kv, weights, weights_b, dprobs, dkv, acc_t = refs[13:]

    def stripes(j):
        return [
            (
                slice((i * XS + x) * SUB, (i * XS + x + 1) * SUB),
                pl.multiple_of(i * ROWS + (2 * x + (half[0] ^ j)) * SUB, SUB),
            )
            for i in range(2)
            for x in range(XS)
        ]

    kv[OWN + CHIP :, :] = jnp.zeros((STEP, 2 * D), kv.dtype)
    for j in range(2):
        for held, place in stripes(j):
            for chip in range(BACK + 1):
                kv[pl.ds(place + OWN - chip * CHIP, SUB), :] = kv_refs[2 * chip + j][held, :]
    dkv[...] = jnp.zeros_like(dkv)
    key_iota = lax.broadcasted_iota(jnp.int32, (TK, LANES), 0)

    def query_tile(qi, _):
        rows = pl.ds(pl.multiple_of(qi * TQ, TQ), TQ)
        q = jnp.concatenate([qdo[rows, j * D : (j + 1) * D] for j in range(GROUP)], axis=0)
        do = jnp.concatenate(
            [qdo[rows, (GROUP + j) * D : (GROUP + j + 1) * D] for j in range(GROUP)], axis=0
        )
        start = start_ref[qi]
        own = own_ref[qi]
        low = span[qi] // 16 * 16
        steps = (span[QTILES + qi] - low) // STEP + 1

        def tiles(step):
            first = low + step * STEP
            return [pl.multiple_of(first + t * TK, 16) for t in range(2)]

        def score(step, top):
            for base in tiles(step):
                keys = pl.ds(base, TK)
                s = dot_nt(kv[keys, :D], q)
                s = jnp.where((key_iota >= start - base) & (key_iota <= own - base), s, MASKED)
                weights[keys, :] = s
                top = jnp.maximum(top, jnp.max(s.reshape(TK // 8, 8, LANES), axis=0))
            return top

        top = lax.fori_loop(0, steps, score, jnp.full((8, LANES), MASKED, jnp.float32))
        top = jnp.max(top, axis=0, keepdims=True) * (SCALE * LOG2E)
        acc_t[...] = jnp.zeros_like(acc_t)

        def weigh(step, total):
            summed = 0.0
            for base in tiles(step):
                keys = pl.ds(base, TK)
                dprobs[keys, :] = dot_nt(kv[keys, D:], do)
                w = jnp.exp2(weights[keys, :] * (SCALE * LOG2E) - top)
                w_b = w.astype(jnp.bfloat16)
                weights_b[keys, :] = w_b
                summed += dot_tn(kv[keys, D:], w_b)
                total = total + jnp.sum(w.reshape(TK // 8, 8, LANES), axis=0)
            acc_t[...] += summed
            return total

        total = lax.fori_loop(0, steps, weigh, jnp.zeros((8, LANES), jnp.float32))
        inverse = 1.0 / jnp.sum(total, axis=0, keepdims=True)
        attended_t = (acc_t[...] * inverse).astype(jnp.bfloat16)
        delta = jnp.sum(
            do.T.astype(jnp.float32) * attended_t.astype(jnp.float32), axis=0, keepdims=True
        )
        inverse = inverse.astype(jnp.bfloat16)
        for j in range(GROUP):
            odq[rows, j * D : (j + 1) * D] = attended_t[:, j * TQ : (j + 1) * TQ].T
        acc_t[...] = jnp.zeros_like(acc_t)

        def grads(step, carry):
            summed = 0.0
            for base in tiles(step):
                keys = pl.ds(base, TK)
                probs = weights_b[keys, :] * inverse
                dscores = probs * (dprobs[keys, :] - delta).astype(jnp.bfloat16)
                summed += dot_tn(kv[keys, :D], dscores)
                dkv[keys, :D] += dot(dscores, q)
                dkv[keys, D:] += dot(probs, do)
            acc_t[...] += summed
            return carry

        lax.fori_loop(0, steps, grads, 0)
        dq_t = (acc_t[...] * SCALE).astype(jnp.bfloat16)
        for j in range(GROUP):
            odq[rows, (GROUP + j) * D : (GROUP + j + 1) * D] = dq_t[:, j * TQ : (j + 1) * TQ].T
        return 0

    lax.fori_loop(0, QTILES, query_tile, 0)
    for j in range(2):
        for held, place in stripes(j):
            for chip in range(BACK + 1):
                part = dkv[pl.ds(place + OWN - chip * CHIP, SUB), :]
                part = jnp.concatenate([part[:, :D] * SCALE, part[:, D:]], axis=1)
                ref = g_refs[2 * chip + j]
                ref[held, :] = part.astype(ref.dtype)


def attention(half, span, start, own, qdo, blocks):
    part = jax.ShapeDtypeStruct((ROWS, 2 * D), jnp.bfloat16)
    kept = jax.ShapeDtypeStruct((ROWS, 2 * D), jnp.float32)
    return pl.pallas_call(
        attention_kernel,
        out_shape=(jax.ShapeDtypeStruct((ROWS, QDO), jnp.bfloat16), kept, kept) + (part,) * 4,
        in_specs=[SMEM, SMEM] + [VMEM] * 9,
        out_specs=(VMEM,) * 7,
        scratch_shapes=[
            pltpu.VMEM((WINDOW, 2 * D), jnp.bfloat16),
            pltpu.VMEM((WINDOW, LANES), jnp.float32),
            pltpu.VMEM((WINDOW, LANES), jnp.bfloat16),
            pltpu.VMEM((WINDOW, LANES), jnp.float32),
            pltpu.VMEM((WINDOW, 2 * D), jnp.float32),
            pltpu.VMEM((D, LANES), jnp.float32),
        ],
        compiler_params=pltpu.CompilerParams(vmem_limit_bytes=44 << 20),
        cost_estimate=pl.CostEstimate(
            flops=6 * 2 * D * ROWS * GROUP * 1200, bytes_accessed=4 << 20, transcendentals=0
        ),
        name="attention",
    )(half, span, start, own, qdo, *blocks)


def query_spans(doc_lengths, place, half):
    ends = jnp.cumsum(doc_lengths)
    row = jnp.arange(ROWS, dtype=jnp.int32)
    stripe = row // SUB
    own = OWN + (stripe // XS) * ROWS + (2 * (stripe % XS) + half) * SUB + row % SUB
    base = (place // 2) * CHIP - OWN
    pos = own + base
    start = jnp.max(jnp.where(ends[None, :] <= pos[:, None], ends[None, :], 0), axis=1) - base
    span = jnp.concatenate([start[::TQ], own[TQ - 1 :: TQ]])

    def tiled(v):
        v = jnp.broadcast_to(v.reshape(QTILES, 1, 1, TQ), (QTILES, 1, GROUP, TQ))
        return v.reshape(QTILES, 1, LANES)

    return span, tiled(start), tiled(own)


CTX = ("y_low", "z", "core")


def exchanged(pieces):
    return lax.all_to_all(pieces, ("core", "x"), split_axis=0, concat_axis=0, tiled=True)


def shifted(shard, by):
    peers = lax.axis_size(CTX)
    pairs = [(i, i + by) for i in range(peers) if 0 <= i + by < peers]
    return lax.ppermute(shard, CTX, pairs)


def half_swapped(shard):
    return lax.ppermute(shard, "y_high", [(0, 1), (1, 0)])


def local(queries, keys, values, output_gradient, doc_lengths):
    place = lax.axis_index(CTX)
    half = lax.axis_index("y_high").astype(jnp.int32)
    own = exchanged(pack(keys, values)).reshape(ROWS, 2 * D)
    theirs = half_swapped(own)
    own1, own2 = shifted(own, 2), shifted(own, 4)
    qdo = exchanged(pack(queries, output_gradient)).reshape(ROWS, QDO)
    theirs1 = shifted(theirs, 2)
    theirs2 = shifted(theirs1, 2)
    span, start, own_pos = query_spans(doc_lengths, place, half)

    blocks = (own, theirs, own1, theirs1, own2, theirs2)
    odq, g0, h0, g1, h1, g2, h2 = attention(half.reshape(1), span, start, own_pos, qdo, blocks)
    h1, h2 = shifted(h1, -2), shifted(h2, -4)
    odq_rows = exchanged(odq.reshape(HEADS, SUB, QDO))
    theirs = (h0 + h1.astype(jnp.float32) + h2.astype(jnp.float32)).astype(jnp.bfloat16)
    got = half_swapped(theirs).astype(jnp.float32)
    g1, g2 = shifted(g1, -2), shifted(g2, -4)
    total = g0 + g1.astype(jnp.float32) + g2.astype(jnp.float32) + got
    odq_rows, total = lax.optimization_barrier((odq_rows, total.astype(jnp.bfloat16)))
    dkv_rows = exchanged(total.reshape(HEADS, SUB, 2 * D))
    return (*unpack(odq_rows), *unpack(dkv_rows))


def solution(mesh):
    mesh = jax.sharding.Mesh(
        mesh.devices.reshape(4, 8, 2, 4, 2), ("y_low", "z", "core", "x", "y_high")
    )
    spec = P(("y_low", "z", "core", "x", "y_high"), None)
    return jax.shard_map(
        local,
        mesh=mesh,
        in_specs=(spec, spec, spec, spec, P()),
        out_specs=(spec, spec, spec, spec),
        check_vma=False,
    )
```

```python
import math

import jax
import jax.numpy as jnp
from jax import lax
from jax.experimental import pallas as pl
from jax.experimental.pallas import tpu as pltpu
from jax.sharding import PartitionSpec as P

HEADS = 8
GROUP = 4
D = 128
ROWS = 384
SUB = 48
XS = 4
CHIP = 2 * ROWS
BACK = 2
OWN = BACK * CHIP
TK = 256
STEP = 2 * TK
WINDOW = OWN + CHIP + STEP
TQ = 128
QTILES = ROWS // TQ
LANES = TQ * GROUP
QDO = 2 * GROUP * D
SCALE = 1.0 / math.sqrt(D)
LOG2E = 1.4426950408889634
MASKED = -1e30

NT = (((1,), (1,)), ((), ()))
TN = (((0,), (0,)), ((), ()))

SMEM = pl.BlockSpec(memory_space=pltpu.SMEM)
VMEM = pl.BlockSpec(memory_space=pltpu.VMEM)


def dot(a, b):
    return jnp.dot(a, b, preferred_element_type=jnp.float32)


def dot_nt(a, b):
    return lax.dot_general(a, b, NT, preferred_element_type=jnp.float32)


def dot_tn(a, b):
    return lax.dot_general(a, b, TN, preferred_element_type=jnp.float32)


def pack_kernel(a_ref, b_ref, out_ref):
    width = a_ref.shape[1] // HEADS
    for head in range(HEADS):
        out_ref[head, :, :width] = a_ref[:, head * width : (head + 1) * width]
        out_ref[head, :, width:] = b_ref[:, head * width : (head + 1) * width]


def pack(a, b):
    width = a.shape[1] // HEADS
    return pl.pallas_call(
        pack_kernel,
        out_shape=jax.ShapeDtypeStruct((HEADS, SUB, 2 * width), jnp.bfloat16),
        in_specs=[VMEM] * 2,
        out_specs=VMEM,
        cost_estimate=pl.CostEstimate(
            flops=0, bytes_accessed=8 * HEADS * SUB * width, transcendentals=0
        ),
        name="pack",
    )(a, b)


def unpack_kernel(got_ref, a_ref, b_ref):
    width = a_ref.shape[1] // HEADS
    for head in range(HEADS):
        a_ref[:, head * width : (head + 1) * width] = got_ref[head, :, :width]
        b_ref[:, head * width : (head + 1) * width] = got_ref[head, :, width:]


def unpack(got):
    width = got.shape[2] // 2
    part = jax.ShapeDtypeStruct((SUB, HEADS * width), jnp.bfloat16)
    return pl.pallas_call(
        unpack_kernel,
        out_shape=(part, part),
        in_specs=[VMEM],
        out_specs=(VMEM, VMEM),
        cost_estimate=pl.CostEstimate(
            flops=0, bytes_accessed=8 * HEADS * SUB * width, transcendentals=0
        ),
        name="unpack",
    )(got)


def attention_kernel(half, span, start_ref, own_ref, qdo, *refs):
    kv_refs, odq, g_refs = refs[:6], refs[6], refs[7:13]
    kv, weights, weights_b, dprobs, dkv, acc_t = refs[13:]

    def stripes(j):
        return [
            (
                slice((i * XS + x) * SUB, (i * XS + x + 1) * SUB),
                pl.multiple_of(i * ROWS + (2 * x + (half[0] ^ j)) * SUB, SUB),
            )
            for i in range(2)
            for x in range(XS)
        ]

    kv[OWN + CHIP :, :] = jnp.zeros((STEP, 2 * D), kv.dtype)
    for j in range(2):
        for held, place in stripes(j):
            for chip in range(BACK + 1):
                kv[pl.ds(place + OWN - chip * CHIP, SUB), :] = kv_refs[2 * chip + j][held, :]
    dkv[...] = jnp.zeros_like(dkv)
    key_iota = lax.broadcasted_iota(jnp.int32, (TK, LANES), 0)

    def query_tile(qi, _):
        rows = pl.ds(pl.multiple_of(qi * TQ, TQ), TQ)
        q = jnp.concatenate([qdo[rows, j * D : (j + 1) * D] for j in range(GROUP)], axis=0)
        do = jnp.concatenate(
            [qdo[rows, (GROUP + j) * D : (GROUP + j + 1) * D] for j in range(GROUP)], axis=0
        )
        start = start_ref[qi]
        own = own_ref[qi]
        low = span[qi] // 16 * 16
        steps = (span[QTILES + qi] - low) // STEP + 1

        def tiles(step):
            first = low + step * STEP
            return [pl.multiple_of(first + t * TK, 16) for t in range(2)]

        def score(step, top):
            for base in tiles(step):
                keys = pl.ds(base, TK)
                s = dot_nt(kv[keys, :D], q)
                s = jnp.where((key_iota >= start - base) & (key_iota <= own - base), s, MASKED)
                weights[keys, :] = s
                top = jnp.maximum(top, jnp.max(s.reshape(TK // 8, 8, LANES), axis=0))
            return top

        top = lax.fori_loop(0, steps, score, jnp.full((8, LANES), MASKED, jnp.float32))
        top = jnp.max(top, axis=0, keepdims=True) * (SCALE * LOG2E)
        acc_t[...] = jnp.zeros_like(acc_t)

        def weigh(step, total):
            summed = 0.0
            for base in tiles(step):
                keys = pl.ds(base, TK)
                dprobs[keys, :] = dot_nt(kv[keys, D:], do)
                w = jnp.exp2(weights[keys, :] * (SCALE * LOG2E) - top)
                w_b = w.astype(jnp.bfloat16)
                weights_b[keys, :] = w_b
                summed += dot_tn(kv[keys, D:], w_b)
                total = total + jnp.sum(w.reshape(TK // 8, 8, LANES), axis=0)
            acc_t[...] += summed
            return total

        total = lax.fori_loop(0, steps, weigh, jnp.zeros((8, LANES), jnp.float32))
        inverse = 1.0 / jnp.sum(total, axis=0, keepdims=True)
        attended_t = (acc_t[...] * inverse).astype(jnp.bfloat16)
        delta = jnp.sum(
            do.T.astype(jnp.float32) * attended_t.astype(jnp.float32), axis=0, keepdims=True
        )
        inverse = inverse.astype(jnp.bfloat16)
        for j in range(GROUP):
            odq[rows, j * D : (j + 1) * D] = attended_t[:, j * TQ : (j + 1) * TQ].T
        acc_t[...] = jnp.zeros_like(acc_t)

        def grads(step, carry):
            summed = 0.0
            for base in tiles(step):
                keys = pl.ds(base, TK)
                probs = weights_b[keys, :] * inverse
                dscores = probs * (dprobs[keys, :] - delta).astype(jnp.bfloat16)
                summed += dot_tn(kv[keys, :D], dscores)
                dkv[keys, :D] += dot(dscores, q)
                dkv[keys, D:] += dot(probs, do)
            acc_t[...] += summed
            return carry

        lax.fori_loop(0, steps, grads, 0)
        dq_t = (acc_t[...] * SCALE).astype(jnp.bfloat16)
        for j in range(GROUP):
            odq[rows, (GROUP + j) * D : (GROUP + j + 1) * D] = dq_t[:, j * TQ : (j + 1) * TQ].T
        return 0

    lax.fori_loop(0, QTILES, query_tile, 0)
    for j in range(2):
        for held, place in stripes(j):
            for chip in range(BACK + 1):
                part = dkv[pl.ds(place + OWN - chip * CHIP, SUB), :]
                part = jnp.concatenate([part[:, :D] * SCALE, part[:, D:]], axis=1)
                ref = g_refs[2 * chip + j]
                ref[held, :] = part.astype(ref.dtype)


def attention(half, span, start, own, qdo, blocks):
    part = jax.ShapeDtypeStruct((ROWS, 2 * D), jnp.bfloat16)
    kept = jax.ShapeDtypeStruct((ROWS, 2 * D), jnp.float32)
    return pl.pallas_call(
        attention_kernel,
        out_shape=(jax.ShapeDtypeStruct((ROWS, QDO), jnp.bfloat16), kept, kept) + (part,) * 4,
        in_specs=[SMEM, SMEM] + [VMEM] * 9,
        out_specs=(VMEM,) * 7,
        scratch_shapes=[
            pltpu.VMEM((WINDOW, 2 * D), jnp.bfloat16),
            pltpu.VMEM((WINDOW, LANES), jnp.float32),
            pltpu.VMEM((WINDOW, LANES), jnp.bfloat16),
            pltpu.VMEM((WINDOW, LANES), jnp.float32),
            pltpu.VMEM((WINDOW, 2 * D), jnp.float32),
            pltpu.VMEM((D, LANES), jnp.float32),
        ],
        compiler_params=pltpu.CompilerParams(vmem_limit_bytes=44 << 20),
        cost_estimate=pl.CostEstimate(
            flops=6 * 2 * D * ROWS * GROUP * 1200, bytes_accessed=4 << 20, transcendentals=0
        ),
        name="attention",
    )(half, span, start, own, qdo, *blocks)


def query_spans(doc_lengths, place, half):
    ends = jnp.cumsum(doc_lengths)
    row = jnp.arange(ROWS, dtype=jnp.int32)
    stripe = row // SUB
    own = OWN + (stripe // XS) * ROWS + (2 * (stripe % XS) + half) * SUB + row % SUB
    base = (place // 2) * CHIP - OWN
    pos = own + base
    start = jnp.max(jnp.where(ends[None, :] <= pos[:, None], ends[None, :], 0), axis=1) - base
    span = jnp.concatenate([start[::TQ], own[TQ - 1 :: TQ]])

    def tiled(v):
        v = jnp.broadcast_to(v.reshape(QTILES, 1, 1, TQ), (QTILES, 1, GROUP, TQ))
        return v.reshape(QTILES, 1, LANES)

    return span, tiled(start), tiled(own)


CTX = ("y_low", "z", "core")


def exchanged(pieces):
    return lax.all_to_all(pieces, ("core", "x"), split_axis=0, concat_axis=0, tiled=True)


def shifted(shard, by):
    peers = lax.axis_size(CTX)
    pairs = [(i, i + by) for i in range(peers) if 0 <= i + by < peers]
    return lax.ppermute(shard, CTX, pairs)


def half_swapped(shard):
    return lax.ppermute(shard, "y_high", [(0, 1), (1, 0)])


def local(queries, keys, values, output_gradient, doc_lengths):
    place = lax.axis_index(CTX)
    half = lax.axis_index("y_high").astype(jnp.int32)
    own = exchanged(pack(keys, values)).reshape(ROWS, 2 * D)
    theirs = half_swapped(own)
    theirs, own1 = lax.optimization_barrier((theirs, shifted(own, 2)))
    own2 = shifted(own1, 2)
    qdo = exchanged(pack(queries, output_gradient)).reshape(ROWS, QDO)
    theirs1 = shifted(theirs, 2)
    theirs2 = shifted(theirs1, 2)
    span, start, own_pos = query_spans(doc_lengths, place, half)

    blocks = (own, theirs, own1, theirs1, own2, theirs2)
    odq, g0, h0, g1, h1, g2, h2 = attention(half.reshape(1), span, start, own_pos, qdo, blocks)
    h1, h2 = shifted(h1, -2), shifted(h2, -4)
    odq_rows = exchanged(odq.reshape(HEADS, SUB, QDO))
    theirs = (h0 + h1.astype(jnp.float32) + h2.astype(jnp.float32)).astype(jnp.bfloat16)
    got = half_swapped(theirs).astype(jnp.float32)
    g1, g2 = shifted(g1, -2), shifted(g2, -4)
    total = g0 + g1.astype(jnp.float32) + g2.astype(jnp.float32) + got
    odq_rows, total = lax.optimization_barrier((odq_rows, total.astype(jnp.bfloat16)))
    dkv_rows = exchanged(total.reshape(HEADS, SUB, 2 * D))
    return (*unpack(odq_rows), *unpack(dkv_rows))


def solution(mesh):
    mesh = jax.sharding.Mesh(
        mesh.devices.reshape(4, 8, 2, 4, 2), ("y_low", "z", "core", "x", "y_high")
    )
    spec = P(("y_low", "z", "core", "x", "y_high"), None)
    return jax.shard_map(
        local,
        mesh=mesh,
        in_specs=(spec, spec, spec, spec, P()),
        out_specs=(spec, spec, spec, spec),
        check_vma=False,
    )
```

```python
import math

import jax
import jax.numpy as jnp
from jax import lax
from jax.experimental import pallas as pl
from jax.experimental.pallas import tpu as pltpu
from jax.sharding import PartitionSpec as P

HEADS = 8
GROUP = 4
D = 128
ROWS = 384
SUB = 48
XS = 4
CHIP = 2 * ROWS
BACK = 2
OWN = BACK * CHIP
TK = 256
STEP = 2 * TK
WINDOW = OWN + CHIP + STEP
TQ = 128
QTILES = ROWS // TQ
LANES = TQ * GROUP
QDO = 2 * GROUP * D
SCALE = 1.0 / math.sqrt(D)
LOG2E = 1.4426950408889634
MASKED = -1e30

NT = (((1,), (1,)), ((), ()))
TN = (((0,), (0,)), ((), ()))

SMEM = pl.BlockSpec(memory_space=pltpu.SMEM)
VMEM = pl.BlockSpec(memory_space=pltpu.VMEM)


def dot(a, b):
    return jnp.dot(a, b, preferred_element_type=jnp.float32)


def dot_nt(a, b):
    return lax.dot_general(a, b, NT, preferred_element_type=jnp.float32)


def dot_tn(a, b):
    return lax.dot_general(a, b, TN, preferred_element_type=jnp.float32)


def pack_kernel(a_ref, b_ref, out_ref):
    width = a_ref.shape[1] // HEADS
    for head in range(HEADS):
        out_ref[head, :, :width] = a_ref[:, head * width : (head + 1) * width]
        out_ref[head, :, width:] = b_ref[:, head * width : (head + 1) * width]


def pack(a, b):
    width = a.shape[1] // HEADS
    return pl.pallas_call(
        pack_kernel,
        out_shape=jax.ShapeDtypeStruct((HEADS, SUB, 2 * width), jnp.bfloat16),
        in_specs=[VMEM] * 2,
        out_specs=VMEM,
        cost_estimate=pl.CostEstimate(
            flops=0, bytes_accessed=8 * HEADS * SUB * width, transcendentals=0
        ),
        name="pack",
    )(a, b)


def unpack_kernel(got_ref, a_ref, b_ref):
    width = a_ref.shape[1] // HEADS
    for head in range(HEADS):
        a_ref[:, head * width : (head + 1) * width] = got_ref[head, :, :width]
        b_ref[:, head * width : (head + 1) * width] = got_ref[head, :, width:]


def unpack(got):
    width = got.shape[2] // 2
    part = jax.ShapeDtypeStruct((SUB, HEADS * width), jnp.bfloat16)
    return pl.pallas_call(
        unpack_kernel,
        out_shape=(part, part),
        in_specs=[VMEM],
        out_specs=(VMEM, VMEM),
        cost_estimate=pl.CostEstimate(
            flops=0, bytes_accessed=8 * HEADS * SUB * width, transcendentals=0
        ),
        name="unpack",
    )(got)


def attention_kernel(half, span, start_ref, own_ref, qdo, *refs):
    kv_refs, odq, g_refs = refs[:6], refs[6], refs[7:13]
    kv, weights, weights_b, dprobs, dkv, acc_t = refs[13:]

    def stripes(j):
        return [
            (
                slice((i * XS + x) * SUB, (i * XS + x + 1) * SUB),
                pl.multiple_of(i * ROWS + (2 * x + (half[0] ^ j)) * SUB, SUB),
            )
            for i in range(2)
            for x in range(XS)
        ]

    kv[OWN + CHIP :, :] = jnp.zeros((STEP, 2 * D), kv.dtype)
    for j in range(2):
        for held, place in stripes(j):
            for chip in range(BACK + 1):
                kv[pl.ds(place + OWN - chip * CHIP, SUB), :] = kv_refs[2 * chip + j][held, :]
    dkv[...] = jnp.zeros_like(dkv)
    key_iota = lax.broadcasted_iota(jnp.int32, (TK, LANES), 0)

    def query_tile(qi, _):
        rows = pl.ds(pl.multiple_of(qi * TQ, TQ), TQ)
        q = jnp.concatenate([qdo[rows, j * D : (j + 1) * D] for j in range(GROUP)], axis=0)
        do = jnp.concatenate(
            [qdo[rows, (GROUP + j) * D : (GROUP + j + 1) * D] for j in range(GROUP)], axis=0
        )
        start = start_ref[qi]
        own = own_ref[qi]
        low = span[qi] // 16 * 16
        steps = (span[QTILES + qi] - low) // STEP + 1

        def tiles(step):
            first = low + step * STEP
            return [pl.multiple_of(first + t * TK, 16) for t in range(2)]

        def score(step, top):
            for base in tiles(step):
                keys = pl.ds(base, TK)
                s = dot_nt(kv[keys, :D], q)
                s = jnp.where((key_iota >= start - base) & (key_iota <= own - base), s, MASKED)
                weights[keys, :] = s
                top = jnp.maximum(top, jnp.max(s.reshape(TK // 8, 8, LANES), axis=0))
            return top

        top = lax.fori_loop(0, steps, score, jnp.full((8, LANES), MASKED, jnp.float32))
        top = jnp.max(top, axis=0, keepdims=True) * (SCALE * LOG2E)
        acc_t[...] = jnp.zeros_like(acc_t)

        def weigh(step, total):
            summed = 0.0
            for base in tiles(step):
                keys = pl.ds(base, TK)
                dprobs[keys, :] = dot_nt(kv[keys, D:], do)
                w = jnp.exp2(weights[keys, :] * (SCALE * LOG2E) - top)
                w_b = w.astype(jnp.bfloat16)
                weights_b[keys, :] = w_b
                summed += dot_tn(kv[keys, D:], w_b)
                total = total + jnp.sum(w.reshape(TK // 8, 8, LANES), axis=0)
            acc_t[...] += summed
            return total

        total = lax.fori_loop(0, steps, weigh, jnp.zeros((8, LANES), jnp.float32))
        inverse = 1.0 / jnp.sum(total, axis=0, keepdims=True)
        attended_t = (acc_t[...] * inverse).astype(jnp.bfloat16)
        delta = jnp.sum(
            do.T.astype(jnp.float32) * attended_t.astype(jnp.float32), axis=0, keepdims=True
        )
        inverse = inverse.astype(jnp.bfloat16)
        for j in range(GROUP):
            odq[rows, j * D : (j + 1) * D] = attended_t[:, j * TQ : (j + 1) * TQ].T
        acc_t[...] = jnp.zeros_like(acc_t)

        def grads(step, carry):
            summed = 0.0
            for base in tiles(step):
                keys = pl.ds(base, TK)
                probs = weights_b[keys, :] * inverse
                dscores = probs * (dprobs[keys, :] - delta).astype(jnp.bfloat16)
                summed += dot_tn(kv[keys, :D], dscores)
                dkv[keys, :D] += dot(dscores, q)
                dkv[keys, D:] += dot(probs, do)
            acc_t[...] += summed
            return carry

        lax.fori_loop(0, steps, grads, 0)
        dq_t = (acc_t[...] * SCALE).astype(jnp.bfloat16)
        for j in range(GROUP):
            odq[rows, (GROUP + j) * D : (GROUP + j + 1) * D] = dq_t[:, j * TQ : (j + 1) * TQ].T
        return 0

    lax.fori_loop(0, QTILES, query_tile, 0)
    for j in range(2):
        for held, place in stripes(j):
            for chip in range(BACK + 1):
                part = dkv[pl.ds(place + OWN - chip * CHIP, SUB), :]
                part = jnp.concatenate([part[:, :D] * SCALE, part[:, D:]], axis=1)
                ref = g_refs[2 * chip + j]
                ref[held, :] = part.astype(ref.dtype)


def attention(half, span, start, own, qdo, blocks):
    part = jax.ShapeDtypeStruct((ROWS, 2 * D), jnp.bfloat16)
    kept = jax.ShapeDtypeStruct((ROWS, 2 * D), jnp.float32)
    return pl.pallas_call(
        attention_kernel,
        out_shape=(jax.ShapeDtypeStruct((ROWS, QDO), jnp.bfloat16), kept, kept) + (part,) * 4,
        in_specs=[SMEM, SMEM] + [VMEM] * 9,
        out_specs=(VMEM,) * 7,
        scratch_shapes=[
            pltpu.VMEM((WINDOW, 2 * D), jnp.bfloat16),
            pltpu.VMEM((WINDOW, LANES), jnp.float32),
            pltpu.VMEM((WINDOW, LANES), jnp.bfloat16),
            pltpu.VMEM((WINDOW, LANES), jnp.float32),
            pltpu.VMEM((WINDOW, 2 * D), jnp.float32),
            pltpu.VMEM((D, LANES), jnp.float32),
        ],
        compiler_params=pltpu.CompilerParams(vmem_limit_bytes=44 << 20),
        cost_estimate=pl.CostEstimate(
            flops=6 * 2 * D * ROWS * GROUP * 1200, bytes_accessed=4 << 20, transcendentals=0
        ),
        name="attention",
    )(half, span, start, own, qdo, *blocks)


def query_spans(doc_lengths, place, half):
    ends = jnp.cumsum(doc_lengths)
    row = jnp.arange(ROWS, dtype=jnp.int32)
    stripe = row // SUB
    own = OWN + (stripe // XS) * ROWS + (2 * (stripe % XS) + half) * SUB + row % SUB
    base = (place // 2) * CHIP - OWN
    pos = own + base
    start = jnp.max(jnp.where(ends[None, :] <= pos[:, None], ends[None, :], 0), axis=1) - base
    span = jnp.concatenate([start[::TQ], own[TQ - 1 :: TQ]])

    def tiled(v):
        v = jnp.broadcast_to(v.reshape(QTILES, 1, 1, TQ), (QTILES, 1, GROUP, TQ))
        return v.reshape(QTILES, 1, LANES)

    return span, tiled(start), tiled(own)


CTX = ("y_low", "z", "core")


def exchanged(pieces):
    return lax.all_to_all(pieces, ("core", "x"), split_axis=0, concat_axis=0, tiled=True)


def shifted(shard, by):
    peers = lax.axis_size(CTX)
    pairs = [(i, i + by) for i in range(peers) if 0 <= i + by < peers]
    return lax.ppermute(shard, CTX, pairs)


def half_swapped(shard):
    return lax.ppermute(shard, "y_high", [(0, 1), (1, 0)])


def local(queries, keys, values, output_gradient, doc_lengths):
    place = lax.axis_index(CTX)
    half = lax.axis_index("y_high").astype(jnp.int32)
    own = exchanged(pack(keys, values)).reshape(ROWS, 2 * D)
    own1 = shifted(own, 2)
    own1, theirs = lax.optimization_barrier((own1, half_swapped(own)))
    own2 = shifted(own1, 2)
    qdo = exchanged(pack(queries, output_gradient)).reshape(ROWS, QDO)
    theirs1 = shifted(theirs, 2)
    theirs2 = shifted(theirs1, 2)
    span, start, own_pos = query_spans(doc_lengths, place, half)

    blocks = (own, theirs, own1, theirs1, own2, theirs2)
    odq, g0, h0, g1, h1, g2, h2 = attention(half.reshape(1), span, start, own_pos, qdo, blocks)
    h1, h2 = shifted(h1, -2), shifted(h2, -4)
    odq_rows = exchanged(odq.reshape(HEADS, SUB, QDO))
    theirs = (h0 + h1.astype(jnp.float32) + h2.astype(jnp.float32)).astype(jnp.bfloat16)
    got = half_swapped(theirs).astype(jnp.float32)
    g1, g2 = shifted(g1, -2), shifted(g2, -4)
    total = g0 + g1.astype(jnp.float32) + g2.astype(jnp.float32) + got
    odq_rows, total = lax.optimization_barrier((odq_rows, total.astype(jnp.bfloat16)))
    dkv_rows = exchanged(total.reshape(HEADS, SUB, 2 * D))
    return (*unpack(odq_rows), *unpack(dkv_rows))


def solution(mesh):
    mesh = jax.sharding.Mesh(
        mesh.devices.reshape(4, 8, 2, 4, 2), ("y_low", "z", "core", "x", "y_high")
    )
    spec = P(("y_low", "z", "core", "x", "y_high"), None)
    return jax.shard_map(
        local,
        mesh=mesh,
        in_specs=(spec, spec, spec, spec, P()),
        out_specs=(spec, spec, spec, spec),
        check_vma=False,
    )
```

```python
import math

import jax
import jax.numpy as jnp
from jax import lax
from jax.experimental import pallas as pl
from jax.experimental.pallas import tpu as pltpu
from jax.sharding import PartitionSpec as P

HEADS = 8
GROUP = 4
D = 128
ROWS = 384
SUB = 48
XS = 4
CHIP = 2 * ROWS
BACK = 2
OWN = BACK * CHIP
TK = 256
STEP = 2 * TK
WINDOW = OWN + CHIP + STEP
TQ = 128
QTILES = ROWS // TQ
LANES = TQ * GROUP
QDO = 2 * GROUP * D
SCALE = 1.0 / math.sqrt(D)
LOG2E = 1.4426950408889634
MASKED = -1e30

NT = (((1,), (1,)), ((), ()))
TN = (((0,), (0,)), ((), ()))

SMEM = pl.BlockSpec(memory_space=pltpu.SMEM)
VMEM = pl.BlockSpec(memory_space=pltpu.VMEM)


def dot(a, b):
    return jnp.dot(a, b, preferred_element_type=jnp.float32)


def dot_nt(a, b):
    return lax.dot_general(a, b, NT, preferred_element_type=jnp.float32)


def dot_tn(a, b):
    return lax.dot_general(a, b, TN, preferred_element_type=jnp.float32)


def pack_kernel(a_ref, b_ref, out_ref):
    width = a_ref.shape[1] // HEADS
    for head in range(HEADS):
        out_ref[head, :, :width] = a_ref[:, head * width : (head + 1) * width]
        out_ref[head, :, width:] = b_ref[:, head * width : (head + 1) * width]


def pack(a, b):
    width = a.shape[1] // HEADS
    return pl.pallas_call(
        pack_kernel,
        out_shape=jax.ShapeDtypeStruct((HEADS, SUB, 2 * width), jnp.bfloat16),
        in_specs=[VMEM] * 2,
        out_specs=VMEM,
        cost_estimate=pl.CostEstimate(
            flops=0, bytes_accessed=8 * HEADS * SUB * width, transcendentals=0
        ),
        name="pack",
    )(a, b)


def unpack_kernel(got_ref, a_ref, b_ref):
    width = a_ref.shape[1] // HEADS
    for head in range(HEADS):
        a_ref[:, head * width : (head + 1) * width] = got_ref[head, :, :width]
        b_ref[:, head * width : (head + 1) * width] = got_ref[head, :, width:]


def unpack(got):
    width = got.shape[2] // 2
    part = jax.ShapeDtypeStruct((SUB, HEADS * width), jnp.bfloat16)
    return pl.pallas_call(
        unpack_kernel,
        out_shape=(part, part),
        in_specs=[VMEM],
        out_specs=(VMEM, VMEM),
        cost_estimate=pl.CostEstimate(
            flops=0, bytes_accessed=8 * HEADS * SUB * width, transcendentals=0
        ),
        name="unpack",
    )(got)


def attention_kernel(half, span, start_ref, own_ref, qdo, *refs):
    kv_refs, odq, g_refs = refs[:6], refs[6], refs[7:13]
    kv, weights, weights_b, dprobs, dkv, acc_t = refs[13:]

    def stripes(j):
        return [
            (
                slice((i * XS + x) * SUB, (i * XS + x + 1) * SUB),
                pl.multiple_of(i * ROWS + (2 * x + (half[0] ^ j)) * SUB, SUB),
            )
            for i in range(2)
            for x in range(XS)
        ]

    kv[OWN + CHIP :, :] = jnp.zeros((STEP, 2 * D), kv.dtype)
    for j in range(2):
        for held, place in stripes(j):
            for chip in range(BACK + 1):
                kv[pl.ds(place + OWN - chip * CHIP, SUB), :] = kv_refs[2 * chip + j][held, :]
    dkv[...] = jnp.zeros_like(dkv)
    key_iota = lax.broadcasted_iota(jnp.int32, (TK, LANES), 0)

    def query_tile(qi, _):
        rows = pl.ds(pl.multiple_of(qi * TQ, TQ), TQ)
        q = jnp.concatenate([qdo[rows, j * D : (j + 1) * D] for j in range(GROUP)], axis=0)
        do = jnp.concatenate(
            [qdo[rows, (GROUP + j) * D : (GROUP + j + 1) * D] for j in range(GROUP)], axis=0
        )
        start = start_ref[qi]
        own = own_ref[qi]
        low = span[qi] // 16 * 16
        steps = (span[QTILES + qi] - low) // STEP + 1

        def tiles(step):
            first = low + step * STEP
            return [pl.multiple_of(first + t * TK, 16) for t in range(2)]

        def score(step, top):
            for base in tiles(step):
                keys = pl.ds(base, TK)
                s = dot_nt(kv[keys, :D], q)
                s = jnp.where((key_iota >= start - base) & (key_iota <= own - base), s, MASKED)
                weights[keys, :] = s
                top = jnp.maximum(top, jnp.max(s.reshape(TK // 8, 8, LANES), axis=0))
            return top

        top = lax.fori_loop(0, steps, score, jnp.full((8, LANES), MASKED, jnp.float32))
        top = jnp.max(top, axis=0, keepdims=True) * (SCALE * LOG2E)
        acc_t[...] = jnp.zeros_like(acc_t)

        def weigh(step, total):
            summed = 0.0
            for base in tiles(step):
                keys = pl.ds(base, TK)
                dprobs[keys, :] = dot_nt(kv[keys, D:], do)
                w = jnp.exp2(weights[keys, :] * (SCALE * LOG2E) - top)
                w_b = w.astype(jnp.bfloat16)
                weights_b[keys, :] = w_b
                summed += dot_tn(kv[keys, D:], w_b)
                total = total + jnp.sum(w.reshape(TK // 8, 8, LANES), axis=0)
            acc_t[...] += summed
            return total

        total = lax.fori_loop(0, steps, weigh, jnp.zeros((8, LANES), jnp.float32))
        inverse = 1.0 / jnp.sum(total, axis=0, keepdims=True)
        attended_t = (acc_t[...] * inverse).astype(jnp.bfloat16)
        delta = jnp.sum(
            do.T.astype(jnp.float32) * attended_t.astype(jnp.float32), axis=0, keepdims=True
        )
        inverse = inverse.astype(jnp.bfloat16)
        for j in range(GROUP):
            odq[rows, j * D : (j + 1) * D] = attended_t[:, j * TQ : (j + 1) * TQ].T
        acc_t[...] = jnp.zeros_like(acc_t)

        def grads(step, carry):
            summed = 0.0
            for base in tiles(step):
                keys = pl.ds(base, TK)
                probs = weights_b[keys, :] * inverse
                dscores = probs * (dprobs[keys, :] - delta).astype(jnp.bfloat16)
                summed += dot_tn(kv[keys, :D], dscores)
                dkv[keys, :D] += dot(dscores, q)
                dkv[keys, D:] += dot(probs, do)
            acc_t[...] += summed
            return carry

        lax.fori_loop(0, steps, grads, 0)
        dq_t = (acc_t[...] * SCALE).astype(jnp.bfloat16)
        for j in range(GROUP):
            odq[rows, (GROUP + j) * D : (GROUP + j + 1) * D] = dq_t[:, j * TQ : (j + 1) * TQ].T
        return 0

    lax.fori_loop(0, QTILES, query_tile, 0)
    for j in range(2):
        for held, place in stripes(j):
            for chip in range(BACK + 1):
                part = dkv[pl.ds(place + OWN - chip * CHIP, SUB), :]
                part = jnp.concatenate([part[:, :D] * SCALE, part[:, D:]], axis=1)
                ref = g_refs[2 * chip + j]
                ref[held, :] = part.astype(ref.dtype)


def attention(half, span, start, own, qdo, blocks):
    part = jax.ShapeDtypeStruct((ROWS, 2 * D), jnp.bfloat16)
    kept = jax.ShapeDtypeStruct((ROWS, 2 * D), jnp.float32)
    return pl.pallas_call(
        attention_kernel,
        out_shape=(jax.ShapeDtypeStruct((ROWS, QDO), jnp.bfloat16), kept, kept) + (part,) * 4,
        in_specs=[SMEM, SMEM] + [VMEM] * 9,
        out_specs=(VMEM,) * 7,
        scratch_shapes=[
            pltpu.VMEM((WINDOW, 2 * D), jnp.bfloat16),
            pltpu.VMEM((WINDOW, LANES), jnp.float32),
            pltpu.VMEM((WINDOW, LANES), jnp.bfloat16),
            pltpu.VMEM((WINDOW, LANES), jnp.float32),
            pltpu.VMEM((WINDOW, 2 * D), jnp.float32),
            pltpu.VMEM((D, LANES), jnp.float32),
        ],
        compiler_params=pltpu.CompilerParams(vmem_limit_bytes=44 << 20),
        cost_estimate=pl.CostEstimate(
            flops=6 * 2 * D * ROWS * GROUP * 1200, bytes_accessed=4 << 20, transcendentals=0
        ),
        name="attention",
    )(half, span, start, own, qdo, *blocks)


def query_spans(doc_lengths, place, half):
    ends = jnp.cumsum(doc_lengths)
    row = jnp.arange(ROWS, dtype=jnp.int32)
    stripe = row // SUB
    own = OWN + (stripe // XS) * ROWS + (2 * (stripe % XS) + half) * SUB + row % SUB
    base = (place // 2) * CHIP - OWN
    pos = own + base
    start = jnp.max(jnp.where(ends[None, :] <= pos[:, None], ends[None, :], 0), axis=1) - base
    span = jnp.concatenate([start[::TQ], own[TQ - 1 :: TQ]])

    def tiled(v):
        v = jnp.broadcast_to(v.reshape(QTILES, 1, 1, TQ), (QTILES, 1, GROUP, TQ))
        return v.reshape(QTILES, 1, LANES)

    return span, tiled(start), tiled(own)


CTX = ("y_low", "z", "core")


def exchanged(pieces):
    return lax.all_to_all(pieces, ("core", "x"), split_axis=0, concat_axis=0, tiled=True)


def shifted(shard, by):
    peers = lax.axis_size(CTX)
    pairs = [(i, i + by) for i in range(peers) if 0 <= i + by < peers]
    return lax.ppermute(shard, CTX, pairs)


def half_swapped(shard):
    return lax.ppermute(shard, "y_high", [(0, 1), (1, 0)])


def local(queries, keys, values, output_gradient, doc_lengths):
    place = lax.axis_index(CTX)
    half = lax.axis_index("y_high").astype(jnp.int32)
    own = exchanged(pack(keys, values)).reshape(ROWS, 2 * D)
    theirs = half_swapped(own)
    theirs, own1 = lax.optimization_barrier((theirs, shifted(own, 2)))
    own2 = shifted(own1, 2)
    qdo = exchanged(pack(queries, output_gradient)).reshape(ROWS, QDO)
    theirs1 = shifted(theirs, 2)
    theirs2 = shifted(theirs1, 2)
    span, start, own_pos = query_spans(doc_lengths, place, half)

    blocks = (own, theirs, own1, theirs1, own2, theirs2)
    odq, g0, h0, g1, h1, g2, h2 = attention(half.reshape(1), span, start, own_pos, qdo, blocks)
    h1 = h1.astype(jnp.float32) + shifted(h2, -2).astype(jnp.float32)
    h1 = shifted(h1.astype(jnp.bfloat16), -2)
    odq_rows = exchanged(odq.reshape(HEADS, SUB, QDO))
    theirs = (h0 + h1.astype(jnp.float32)).astype(jnp.bfloat16)
    got = half_swapped(theirs).astype(jnp.float32)
    g1 = g1.astype(jnp.float32) + shifted(g2, -2).astype(jnp.float32)
    g1 = shifted(g1.astype(jnp.bfloat16), -2)
    total = g0 + g1.astype(jnp.float32) + got
    odq_rows, total = lax.optimization_barrier((odq_rows, total.astype(jnp.bfloat16)))
    dkv_rows = exchanged(total.reshape(HEADS, SUB, 2 * D))
    return (*unpack(odq_rows), *unpack(dkv_rows))


def solution(mesh):
    mesh = jax.sharding.Mesh(
        mesh.devices.reshape(4, 8, 2, 4, 2), ("y_low", "z", "core", "x", "y_high")
    )
    spec = P(("y_low", "z", "core", "x", "y_high"), None)
    return jax.shard_map(
        local,
        mesh=mesh,
        in_specs=(spec, spec, spec, spec, P()),
        out_specs=(spec, spec, spec, spec),
        check_vma=False,
    )
```
